32 devices in a mesh: dp: 8 (over z, y), rep: 4 (over x, core).
Axes of the slice: x: 2, y: 2, z: 4, core: 2. Of those that a mesh axis runs over, the one named last changes fastest.
Arguments:
- q_raw: bfloat16 [3, 96, 8192], P(None, 'dp', 'rep'), may hold values from -16 to 16
- k_raw: bfloat16 [3, 96, 512], P(None, 'dp', 'rep'), may hold values from -8 to 8
- v_raw: bfloat16 [3, 96, 512], P(None, 'dp', 'rep'), may hold values from -6 to 6
- q_gain: float32 [128], replicated, may hold values from 0.6 to 5.5
- k_gain: float32 [128], replicated, may hold values from 0.6 to 5.5
- kv_pool: bfloat16 [384, 64, 2, 512], P('dp', None, None, 'rep'), may hold values from -6 to 6
- page_table: int32 [96, 4], P('dp'), may hold values from 0 to 47, as said below
- cache_len: int32 [96], P('dp'), may hold values from 1 to 253, as said below
- out_pages: int32 [64], P('dp'), may hold values from 0 to 47, as said below
- in_slots: int32 [64], P('dp'), may hold values from 0 to 47, as said below
- hidden_in: bfloat16 [3, 96, 4096], P(None, 'dp', 'rep'), may hold values from -48 to 48
- ln_gain: float32 [4096], replicated, may hold values from 0.1 to 1.9
- route_ids: int32 [3, 96, 8], P(None, 'dp'), may hold values from 0 to 63, all different within a row; in each aligned block of 12 rows (0 to 11, 12 to 23, ..., all dimensions but the last counted through in order) at most 2 rows name the same one
- route_logits: float32 [3, 96, 8], P(None, 'dp'), may hold values from -4 to 4
- w_gate: bfloat16 [128, 4096, 512], P('dp', None, 'rep'), may hold values from -0.09375 to 0.09375
- w_up: bfloat16 [128, 4096, 512], P('dp', None, 'rep'), may hold values from -0.09375 to 0.09375
- w_down: bfloat16 [128, 512, 4096], P('dp', None, 'rep'), may hold values from -0.1875 to 0.1875
Outputs:
- attn_out: bfloat16 [3, 96, 8192], P(None, 'dp', 'rep')
- moe_out: bfloat16 [3, 96, 4096], P(None, 'dp', 'rep')
The draws below stay inside these ranges and needn't reach their ends.
Inputs may be any that keep to these rules, and one draw needn't show every extreme that they name: `route_ids`: each row names 8 different experts; in each step the 12 rows of one dp index name no expert more than 2 times, a bound that some block reaches. `page_table`: the 12 rows of one dp index hold each page number of that index once. `cache_len`: the first request holds the most. `out_pages`: the 8 entries of one dp index are different pages. `in_slots`: the 8 entries of one dp index are different pages.
All inputs are finite; a program needn't handle non-finite values.
Results may differ from the reference program's by a relative error of at most 0.008.
Values may be sent and summed in bfloat16 or wider, within the bound.
No kernel may reach another device: no remote copies, remote signals or barrier semaphores. Data moves between devices by JAX's collectives and lax.ppermute only.
A program may use at most 128 MiB of HBM per device.

```python
import math
import jax
import jax.numpy as jnp
import numpy as np
from jax import lax

D = 4096
HEADS = 64
KV_HEADS = 4
HEAD_DIM = 128
EXPERTS = 64
TOP_K = 8
FF = 1024
STEPS = 3
REQ_DEV = 12
PAGE = 64
PAGES_REQ = 4
MIGRATE = 8
CAPACITY = 2
POOL = 48
REQUESTS = 96
PAGES_ALL = 384
SHARDS = 128
N_DP = 8


def key_base(key):
    return jax.random.normal(key, (STEPS, REQUESTS, KV_HEADS * HEAD_DIM), jnp.float32)


def draw_k_raw(key, part):
    base = key_base(key)
    return jnp.clip(base, -8.0, 8.0).astype(jnp.bfloat16)


def draw_q_raw(key, part):
    key = jax.random.fold_in(key, 12)
    first_key = jax.random.fold_in(key, 0)
    values = jax.random.normal(first_key, (STEPS, REQUESTS, HEADS * HEAD_DIM), jnp.float32)
    return jnp.clip(values, -16.0, 16.0).astype(jnp.bfloat16)


def draw_q_gain(key, part):
    key = jax.random.fold_in(key, 13)
    return jax.random.uniform(key, (HEAD_DIM,), jnp.float32, 0.6, 1.6)


def draw_k_gain(key, part):
    key = jax.random.fold_in(key, 14)
    return jax.random.uniform(key, (HEAD_DIM,), jnp.float32, 0.6, 1.6)


def draw_hidden_in(key, part):
    key = jax.random.fold_in(key, 15)
    first_key = jax.random.fold_in(key, 0)
    rising = 3.0 ** (jnp.arange(D, dtype=jnp.float32) / D)
    values = jax.random.normal(first_key, (STEPS, REQUESTS, D), jnp.float32) * rising
    return jnp.clip(values, -48.0, 48.0).astype(jnp.bfloat16)


def rank_orders(key):
    ranks = REQUESTS // REQ_DEV
    keys = jax.random.split(key, ranks)
    return jax.vmap(lambda single: jax.random.permutation(single, POOL))(keys).astype(jnp.int32)


def draw_page_table(key, part):
    key = jax.random.fold_in(key, 16)
    return rank_orders(key).reshape(REQUESTS, PAGES_REQ)


def draw_out_pages(key, part):
    key = jax.random.fold_in(key, 17)
    return rank_orders(key)[:, :MIGRATE].reshape(-1)


def draw_in_slots(key, part):
    key = jax.random.fold_in(key, 18)
    return rank_orders(key)[:, :MIGRATE].reshape(-1)


def draw_cache_len(key, part):
    key = jax.random.fold_in(key, 19)
    longest = PAGES_REQ * PAGE - STEPS
    lengths = jax.random.randint(key, (REQUESTS,), 1, longest + 1, jnp.int32)
    return lengths.at[0].set(longest)


def block_scale(stream_key, extent, shards, low, top_value):
    level = 1.0
    for axis_at, parts in shards:
        steps = jax.random.uniform(jax.random.fold_in(jax.random.fold_in(stream_key, 6), axis_at), (parts,), jnp.float32, low / len(shards), top_value / len(shards))
        level = level * jnp.repeat(jnp.exp(steps), extent[axis_at] // parts).reshape((-1,) + (1,) * (len(extent) - 1 - axis_at))
    return level


def deal_out(own_key, own, number, rows, number_of, top, limit, lean):
    order = jax.random.permutation(own_key, number_of)
    crowded, ordinary = shares(number_of, rows * top, limit, lean, True), shares(number_of, rows * top, limit, lean, False)
    places = jnp.arange(number_of)

    def named(tallies, offset_by):
        used = int((tallies > 0).sum())
        fixed = max(1, used // 4)
        passed = fixed + (places - fixed + offset_by * (used - fixed)) % max(1, number_of - fixed)
        return jnp.zeros((number_of,), jnp.int32).at[order[jnp.where(places < fixed, places, passed)]].set(jnp.asarray(tallies, jnp.int32))

    tallies = jnp.where(number % 4 == 0, named(crowded, number // 4), named(ordinary, number - number // 4 - 1))
    mixed = jax.random.permutation(jax.random.fold_in(own, 3), number_of)
    donor, taker = mixed[0:number_of // 2 * 2:2], mixed[1:number_of // 2 * 2:2]
    room = jnp.minimum(tallies[donor] - 1, limit - tallies[taker]) // 2
    room = jnp.where((donor == order[0]) | (taker == order[0]) | (tallies[taker] == 0), 0, jnp.maximum(room, 0))
    passed = jax.random.randint(jax.random.fold_in(own, 4), (number_of // 2,), 0, 1 << 20) % (room + 1)
    tallies = tallies.at[donor].add(-passed).at[taker].add(passed)
    labels = jnp.searchsorted(jnp.cumsum(tallies), jnp.arange(rows * top), side="right").astype(jnp.int32)
    table = labels.reshape(top, rows).T
    table = table[jax.random.permutation(jax.random.fold_in(own, 1), rows)]
    offset_by = jax.random.randint(jax.random.fold_in(own, 2), (rows, 1), 0, top)
    return jnp.take_along_axis(table, (jnp.arange(top)[None, :] + offset_by) % top, axis=1)


def shares(count, total, bound, skew, full):
    portions = [(1 << 20) // math.isqrt(rank ** skew) + 1 for rank in range(1, count + 1)]
    largest = bound if full else min(bound, max(-(-total // count), total * portions[0] // sum(portions)))
    least = 1 if total - largest >= count - 1 else 0
    counts, surplus = [largest] + [least] * (count - 1), total - largest - least * (count - 1)
    while surplus > 0:
        candidates = [i for i in range(1, count) if counts[i] < largest] or [i for i in range(1, count) if counts[i] < bound]
        whole, left = sum([portions[i] for i in candidates]), surplus
        for i in candidates:
            more = min(bound - counts[i], max(1, left * portions[i] // whole), surplus)
            counts[i] = counts[i] + more
            surplus = surplus - more
    return np.array(counts)


def gaussian(stream_key, extent, spread, limit, cuts=(), kind=jnp.bfloat16):
    drawn = spread * jax.random.normal(stream_key, extent, jnp.float32)
    if cuts:
        drawn = drawn * block_scale(stream_key, extent, cuts, -0.22, 0.18)
    return jnp.clip(drawn, -limit, limit).astype(kind)


def setup_inputs(seed: int = 0) -> dict:
    arg_keys = jax.random.split(jax.random.key(seed), 18)
    q_raw = draw_q_raw(jax.random.fold_in(arg_keys[17], 71), 0)
    k_raw = draw_k_raw(jax.random.fold_in(arg_keys[17], 71), 0)
    v_raw = gaussian(arg_keys[2], (STEPS, REQUESTS, KV_HEADS * HEAD_DIM), 1.0, 6.0, ((1, 8), (2, 4)))
    q_gain = draw_q_gain(jax.random.fold_in(arg_keys[17], 71), 0)
    k_gain = draw_k_gain(jax.random.fold_in(arg_keys[17], 71), 0)
    kv_pool = gaussian(arg_keys[5], (PAGES_ALL, PAGE, 2, KV_HEADS * HEAD_DIM), 1.0, 6.0, ((0, 8), (3, 4)))
    page_table = draw_page_table(jax.random.fold_in(arg_keys[17], 71), 0)
    cache_len = draw_cache_len(jax.random.fold_in(arg_keys[17], 71), 0)
    out_pages = draw_out_pages(jax.random.fold_in(arg_keys[17], 71), 0)
    in_slots = draw_in_slots(jax.random.fold_in(arg_keys[17], 71), 0)
    hidden_in = draw_hidden_in(jax.random.fold_in(arg_keys[17], 71), 0)
    ln_gain = jnp.clip(1.0 + 0.18 * jax.random.normal(arg_keys[11], (D,), jnp.float32), 0.1, 1.9)
    route_ids_keys = jax.random.split(jax.random.fold_in(arg_keys[12], 1), STEPS * REQUESTS // REQ_DEV)
    route_ids_turns = jax.random.permutation(jax.random.fold_in(arg_keys[12], 3), STEPS * REQUESTS // REQ_DEV)
    route_ids = jax.vmap(lambda own, number: deal_out(jax.random.fold_in(arg_keys[12], 2), own, number, REQ_DEV, EXPERTS, TOP_K, CAPACITY, 2))(route_ids_keys, route_ids_turns).reshape((STEPS, REQUESTS, TOP_K))
    route_logits = gaussian(arg_keys[13], (STEPS, REQUESTS, TOP_K), 1.0, 4.0, ((1, 8),), jnp.float32)
    w_gate = gaussian(arg_keys[14], (SHARDS, D, FF // 2), D ** -0.5, 0.09375, ((0, 8), (2, 4)))
    w_up = gaussian(arg_keys[15], (SHARDS, D, FF // 2), D ** -0.5, 0.09375, ((0, 8), (2, 4)))
    w_down = gaussian(arg_keys[16], (SHARDS, FF // 2, D), FF ** -0.5, 0.1875, ((0, 8), (2, 4)))
    return {"q_raw": q_raw, "k_raw": k_raw, "v_raw": v_raw, "q_gain": q_gain, "k_gain": k_gain, "kv_pool": kv_pool, "page_table": page_table, "cache_len": cache_len, "out_pages": out_pages, "in_slots": in_slots, "hidden_in": hidden_in, "ln_gain": ln_gain, "route_ids": route_ids, "route_logits": route_logits, "w_gate": w_gate, "w_up": w_up, "w_down": w_down}


EPS = 1e-06
THETA = 1000000.0

def head_norm(values, gain):
    mean_square = lax.optimization_barrier(jnp.mean(values * values, axis=-1, keepdims=True))
    return values * lax.rsqrt(mean_square + EPS) * gain

def rotate(values, position):
    half_dim = values.shape[-1] // 2
    exponent = jnp.arange(half_dim, dtype=jnp.float32) * (2.0 / values.shape[-1])
    frequency = THETA ** (-exponent)
    angle = position.astype(jnp.float32)[:, None] * frequency[None, :]
    cosine = jnp.cos(angle)[:, None, :]
    sine_part = jnp.sin(angle)[:, None, :]
    first_half = values[..., :half_dim]
    second_half = values[..., half_dim:]
    return jnp.concatenate([first_half * cosine - second_half * sine_part, second_half * cosine + first_half * sine_part], axis=-1)

def attend(context, lengths, queries_in, keys_in, values_in, q_gain, k_gain):
    row_count, span_len, _, kv_width = context.shape
    kv_count = kv_width // HEAD_DIM
    q_count = queries_in.shape[-1] // HEAD_DIM
    groups = q_count // kv_count
    places = jnp.arange(span_len, dtype=jnp.int32)
    scaling = 1.0 / math.sqrt(HEAD_DIM)
    results = []
    for step_index in range(STEPS):
        position = lengths + step_index
        queries = queries_in[step_index].astype(jnp.float32).reshape(row_count, q_count, HEAD_DIM)
        queries = rotate(head_norm(queries, q_gain), position).astype(jnp.bfloat16)
        new_keys = keys_in[step_index].astype(jnp.float32).reshape(row_count, kv_count, HEAD_DIM)
        new_keys = rotate(head_norm(new_keys, k_gain), position).astype(jnp.bfloat16)
        fresh_rows = jnp.stack([new_keys.reshape(row_count, kv_width), values_in[step_index]], axis=1)
        landing = (places[None, :] == position[:, None])[:, :, None, None]
        context = jnp.where(landing, fresh_rows[:, None, :, :], context)
        key_rows = context[:, :, 0, :].reshape(row_count, span_len, kv_count, HEAD_DIM).astype(jnp.float32)
        value_rows = context[:, :, 1, :].reshape(row_count, span_len, kv_count, HEAD_DIM).astype(jnp.float32)
        grouped = queries.astype(jnp.float32).reshape(row_count, kv_count, groups, HEAD_DIM)
        scores = jnp.einsum('rhgd,rshd->rhgs', grouped, key_rows) * scaling
        valid = (places[None, :] <= position[:, None])[:, None, None, :]
        scores = jnp.where(valid, scores, -1e+30)
        row_top = lax.optimization_barrier(jnp.max(scores, axis=-1, keepdims=True))
        expos = jnp.where(valid, jnp.exp(scores - row_top), 0.0)
        probs = (expos / lax.optimization_barrier(jnp.sum(expos, axis=-1, keepdims=True))).astype(jnp.bfloat16)
        mixed = jnp.einsum('rhgs,rshd->rhgd', probs.astype(jnp.float32), value_rows)
        results.append(mixed.reshape(row_count, q_count * HEAD_DIM).astype(jnp.bfloat16))
    return jnp.stack(results)

def place(route_ids):
    flat_ids = route_ids.reshape(route_ids.shape[0], -1)
    hot_table = (flat_ids[:, :, None] == jnp.arange(EXPERTS, dtype=jnp.int32)[None, None, :]).astype(jnp.int32)
    before = jnp.cumsum(hot_table, axis=1) - hot_table
    return lax.optimization_barrier(jnp.sum(before * hot_table, axis=2)).reshape(route_ids.shape)

def reference(q_raw, k_raw, v_raw, q_gain, k_gain, kv_pool, page_table, cache_len, out_pages, in_slots, hidden_in, ln_gain, route_ids, route_logits, w_gate, w_up, w_down):
    ranks = N_DP
    kv_width = kv_pool.shape[-1]
    pool = kv_pool.reshape(ranks, POOL, PAGE, 2, kv_width)
    leaving = jax.vmap(lambda pages, chosen: pages[chosen])(pool, out_pages.reshape(ranks, MIGRATE))
    arriving = jnp.roll(leaving, ranks // 2, axis=0)
    pool = jax.vmap(lambda pages, chosen, incoming: pages.at[chosen].set(incoming))(pool, in_slots.reshape(ranks, MIGRATE), arriving)

    def per_rank(array_in):
        return array_in.reshape(STEPS, ranks, REQ_DEV, -1).transpose(1, 0, 2, 3)

    def one_rank(inputs):
        pages, table, lengths, queries, new_keys, new_values = inputs
        context = pages[table].reshape(REQ_DEV, PAGES_REQ * PAGE, 2, kv_width)
        return attend(context, lengths, queries, new_keys, new_values, q_gain, k_gain)
    attended = lax.map(one_rank, (pool, page_table.reshape(ranks, REQ_DEV, PAGES_REQ), cache_len.reshape(ranks, REQ_DEV), per_rank(q_raw), per_rank(k_raw), per_rank(v_raw)))
    attn_out = attended.transpose(1, 0, 2, 3).reshape(STEPS, REQUESTS, HEADS * HEAD_DIM)
    values = hidden_in.astype(jnp.float32)
    mean_square = lax.optimization_barrier(jnp.mean(values * values, axis=-1, keepdims=True))
    normed = (values * lax.rsqrt(mean_square + EPS) * ln_gain).astype(jnp.bfloat16)
    normed_rank = per_rank(normed)
    ids_rank = per_rank(route_ids)
    slots = jax.vmap(place)(ids_rank)
    section_index = jnp.broadcast_to(jnp.arange(STEPS, dtype=jnp.int32)[:, None, None], (STEPS, REQ_DEV, TOP_K))

    def fill(normed_one, ids_one, slot_one):
        buffer = jnp.zeros((EXPERTS, STEPS, CAPACITY, D), jnp.bfloat16)
        spread_rows = jnp.broadcast_to(normed_one[:, :, None, :], (STEPS, REQ_DEV, TOP_K, D))
        return buffer.at[ids_one, section_index, slot_one].set(spread_rows)
    buffers = jax.vmap(fill)(normed_rank, ids_rank, slots)

    def expert_pass(expert):
        rows_in = buffers[:, expert].reshape(-1, D)
        outputs = []
        for half_index in range(2):
            shard = half_index * EXPERTS + expert
            gate = jnp.dot(rows_in, w_gate[shard], preferred_element_type=jnp.float32)
            upper = jnp.dot(rows_in, w_up[shard], preferred_element_type=jnp.float32)
            hidden = (jax.nn.silu(gate) * upper).astype(jnp.bfloat16)
            outputs.append(jnp.dot(hidden, w_down[shard], preferred_element_type=jnp.float32).astype(jnp.bfloat16))
        return jnp.stack(outputs)
    expert_out = lax.map(expert_pass, jnp.arange(EXPERTS, dtype=jnp.int32))
    expert_out = expert_out.reshape(EXPERTS, 2, ranks, STEPS, CAPACITY, D)

    def combine(inputs):
        rank_index, ids_one, slot_one, logits_one = inputs
        picked = expert_out[:, :, rank_index]
        first_half = picked[ids_one, 0, section_index, slot_one].astype(jnp.float32)
        second_half = picked[ids_one, 1, section_index, slot_one].astype(jnp.float32)
        weights = jax.nn.softmax(logits_one, axis=-1)
        return lax.optimization_barrier(jnp.sum(weights[..., None] * (first_half + second_half), axis=2)).astype(jnp.bfloat16)
    mixed = lax.map(combine, (jnp.arange(ranks, dtype=jnp.int32), ids_rank, slots, per_rank(route_logits)))
    moe_out = mixed.transpose(1, 0, 2, 3).reshape(STEPS, REQUESTS, D)
    return (attn_out, moe_out)
```

```python
import functools
import math

import jax
import jax.numpy as jnp
import numpy as np
from jax import lax
from jax.experimental import pallas as pl
from jax.experimental.pallas import tpu as pltpu
from jax.sharding import PartitionSpec as P

D = 4096
HEAD_DIM = 128
EXPERTS = 64
STEPS = 3
CAPACITY = 2
TOP_K = 8
SLAB = 16
LANES = 128
PIECES = LANES // SLAB

EPS = 1e-06
THETA = 1000000.0

BF16 = jnp.bfloat16
F32 = jnp.float32
ANY = pl.BlockSpec(memory_space=pl.ANY)
VMEM = pl.BlockSpec(memory_space=pltpu.VMEM)
SMEM = pl.BlockSpec(memory_space=pltpu.SMEM)


def place(route_ids):
    flat_ids = route_ids.reshape(route_ids.shape[0], -1)
    hot_table = (
        flat_ids[:, :, None] == jnp.arange(EXPERTS, dtype=jnp.int32)[None, None, :]
    ).astype(jnp.int32)
    before = jnp.cumsum(hot_table, axis=1) - hot_table
    return jnp.sum(before * hot_table, axis=2).reshape(route_ids.shape)


def attention_kernel(
    first, count, table, lengths, slots_in, q_ref, k_ref, v_ref, qg_ref, kg_ref, speed_ref, pool_ref, new_ref, *refs
):
    out_ref, source, angles = refs[-3:]
    pool_count = pool_ref.shape[0]
    new_count = new_ref.shape[0]
    row_count = q_ref.shape[1]
    page_count = table.shape[0]
    page_rows = pool_ref.shape[1]
    heads = q_ref.shape[2] // HEAD_DIM
    if first:
        out_ref[...] = refs[0][...]
    for slot in range(pool_count):
        source[slot] = -1
    for at in range(new_count):
        source[slots_in[at]] = at

    def page_of(slot):
        at = source[slot]
        return jnp.where(at >= 0, new_ref[jnp.maximum(at, 0)], pool_ref[slot])

    scaling = 1.0 / math.sqrt(HEAD_DIM)
    angles[...] = jnp.zeros(angles.shape, F32)
    for step in range(STEPS):
        for row in range(row_count):
            position = (lengths[row] + step).astype(F32)
            angles[pl.ds(step * row_count + row, 1), :] = speed_ref[...] * position
    first_half = lax.broadcasted_iota(jnp.int32, angles.shape, 1) < HEAD_DIM // 2
    cosines = jnp.cos(angles[...])
    sines = jnp.sin(angles[...])
    sines = jnp.where(first_half, -sines, sines)

    def turned(values, gain, cosine, sine):
        mean_square = jnp.mean(values * values, axis=-1, keepdims=True)
        normed = values * lax.rsqrt(mean_square + EPS) * gain
        return (normed * cosine + pltpu.roll(normed, HEAD_DIM // 2, 1) * sine).astype(BF16)

    width = page_count * page_rows
    column = lax.broadcasted_iota(jnp.int32, (STEPS * heads, width), 1)
    fresh_column = lax.broadcasted_iota(jnp.int32, (STEPS * heads, STEPS), 1)
    fresh_row = lax.broadcasted_iota(jnp.int32, (STEPS * heads, STEPS), 0) // heads
    for row in range(first, first + count):
        queries = []
        keys = []
        for step in range(STEPS):
            at = step * row_count + row
            cosine = cosines[at : at + 1]
            sine = sines[at : at + 1]
            raw = q_ref[step, pl.ds(row, 1), :].astype(F32)
            raw = jnp.concatenate(
                [raw[:, h * HEAD_DIM : (h + 1) * HEAD_DIM] for h in range(heads)], axis=0
            )
            queries.append(turned(raw, qg_ref[...], cosine, sine))
            keys.append(turned(k_ref[step, pl.ds(row, 1), :].astype(F32), kg_ref[...], cosine, sine))
        queries = jnp.concatenate(queries, axis=0)
        context = jnp.concatenate(
            [page_of(table[page, row]) for page in range(page_count)], axis=0
        )
        contract = (((1,), (1,)), ((), ()))
        scores = lax.dot_general(queries, context, contract, preferred_element_type=F32) * scaling
        valid = (column < 2 * lengths[row]) & (column % 2 == 0)
        scores = jnp.where(valid, scores, -1e30)
        fresh = jnp.concatenate(
            [
                jnp.sum(queries.astype(F32) * key.astype(F32), axis=-1, keepdims=True)
                for key in keys
            ],
            axis=1,
        )
        fresh = jnp.where(fresh_column <= fresh_row, fresh * scaling, -1e30)
        top = jnp.maximum(
            jnp.max(scores, axis=-1, keepdims=True), jnp.max(fresh, axis=-1, keepdims=True)
        )
        expos = jnp.where(valid, jnp.exp(scores - top), 0.0)
        fresh = jnp.where(fresh_column <= fresh_row, jnp.exp(fresh - top), 0.0)
        total = jnp.sum(expos, axis=-1, keepdims=True) + jnp.sum(fresh, axis=-1, keepdims=True)
        probs = pltpu.roll(expos / total, 1, 1).astype(BF16)
        mixed = jnp.dot(probs, context, preferred_element_type=F32)
        fresh = (fresh / total).astype(BF16).astype(F32)
        for step in range(STEPS):
            value = v_ref[step, pl.ds(row, 1), :].astype(F32)
            mixed = mixed + fresh[:, step : step + 1] * value
        for step in range(STEPS):
            part = mixed[step * heads : (step + 1) * heads]
            out_ref[step, pl.ds(row, 1), :] = jnp.concatenate(
                [part[h : h + 1] for h in range(heads)], axis=1
            ).astype(BF16)


def attention(
    arriving, q_raw, k_raw, v_raw, q_gain, k_gain, pool, page_table, cache_len, in_slots, first, count,
    so_far=None, tie=None
):
    extra = [x for x in (so_far, tie) if x is not None]
    row_count = q_raw.shape[1]
    exponent = np.arange(HEAD_DIM // 2, dtype=np.float32) * np.float32(2.0 / HEAD_DIM)
    speed = np.power(np.float32(THETA), -exponent)
    speed = jnp.asarray(np.concatenate([speed, speed])[None], F32)
    scratch = [
        pltpu.SMEM((pool.shape[0],), jnp.int32),
        pltpu.VMEM((-(-STEPS * row_count // 8) * 8, HEAD_DIM), F32),
    ]
    return pl.pallas_call(
        functools.partial(attention_kernel, first, count),
        out_shape=jax.ShapeDtypeStruct(q_raw.shape, BF16),
        in_specs=[SMEM] * 3 + [VMEM] * (8 + (so_far is not None)) + [ANY] * (tie is not None),
        out_specs=VMEM,
        scratch_shapes=scratch,
        compiler_params=pltpu.CompilerParams(vmem_limit_bytes=12 << 20),
        cost_estimate=pl.CostEstimate(
            flops=400_000_000, bytes_accessed=8_000_000, transcendentals=400_000
        ),
        name="attention",
    )(
        page_table.T, cache_len, in_slots, q_raw, k_raw, v_raw, q_gain[None], k_gain[None], speed,
        pool, arriving, *extra,
    )


def swap(x, axis, bits):
    size = lax.axis_size(axis)
    return lax.ppermute(x, axis, [(i, i ^ bits) for i in range(size)])


def in_hbm(x):
    return pltpu.with_memory_space_constraint(x, pltpu.HBM)


def block_kernel(
    here, out_pages, ids_hbm, logits_hbm, hidden_hbm, gain_hbm, pool_ref, out_ref, leaving, ids_ref,
    logits_ref, hidden_ref, gain_ref, page_ids, wide, sems, page_sems,
):
    rank = here[0]
    row_count = ids_ref.shape[2]
    width = out_ref.shape[1]
    part = pl.ds(pl.multiple_of(here[1] * width, width), width)
    copies = [
        pltpu.make_async_copy(source, target, sems.at[at])
        for at, (source, target) in enumerate(
            (
                (ids_hbm, ids_ref),
                (logits_hbm, logits_ref),
                (hidden_hbm, hidden_ref),
                (gain_hbm.at[:, part], gain_ref),
                (out_pages, page_ids),
            )
        )
    ]
    for copy in copies:
        copy.start()
    lane_at = lax.broadcasted_iota(jnp.int32, (TOP_K, LANES), 1)
    wide[...] = jnp.zeros(wide.shape, F32)
    copies[4].wait()
    pages = [
        pltpu.make_async_copy(pool_ref.at[page_ids[at]], leaving.at[at], page_sems.at[at])
        for at in range(leaving.shape[0])
    ]
    for copy in pages:
        copy.start()
    copies[0].wait()
    copies[1].wait()
    groups = [jnp.zeros((4, LANES), F32) for _ in range(4)]

    def put(piece, value):
        turned = pltpu.roll(value, ((piece + rank) % PIECES) * SLAB, 1)
        groups[piece // PIECES] += turned

    for step in range(STEPS):
        wide[step, 0, :, :row_count] = ids_ref[step].astype(F32)
        wide[step, 1, :, :row_count] = logits_ref[step]
        ids = wide[step, 0]
        logits = wide[step, 1]
        expos = jnp.exp(logits - jnp.max(logits, axis=0, keepdims=True))
        weights = expos / jnp.sum(expos, axis=0, keepdims=True)
        high = weights.astype(BF16).astype(F32)
        slot = jnp.zeros((TOP_K, LANES), F32)
        for back in range(1, row_count):
            earlier = pltpu.roll(ids, back, 1)
            for k in range(TOP_K):
                same = (ids == earlier[k : k + 1]) & (lane_at >= back)
                slot = slot + jnp.where(same, 1.0, 0.0)
        for at, value in enumerate((ids * CAPACITY + slot + 1.0, high, weights - high)):
            value = jnp.where(lane_at < row_count, value, 0.0)
            for side in range(2):
                put((2 * step + side) * 3 + at, value[4 * side : 4 * side + 4])
    copies[2].wait()
    copies[3].wait()
    gain = gain_ref[...]
    row_at = lax.broadcasted_iota(jnp.int32, (row_count, LANES), 0)
    column_at = lax.broadcasted_iota(jnp.int32, (row_count, LANES), 1)
    rows = []
    for step in range(STEPS):
        values = hidden_ref[step].astype(F32)
        square = jnp.sum(values * values, axis=-1, keepdims=True)
        rest = jnp.sum(jnp.where(row_at == column_at, square, 0.0), axis=0, keepdims=True)
        rest = jnp.concatenate([rest, jnp.zeros((3, LANES), F32)], axis=0)
        for at in range(3):
            high = rest.astype(BF16).astype(F32)
            put(18 + 3 * step + at, high)
            rest = rest - high
        rows.append(values * gain)
    groups.append(jnp.zeros((4, width - 4 * LANES), F32))
    out_ref[...] = jnp.concatenate(rows + [jnp.concatenate(groups, axis=1)], axis=0).astype(BF16)
    for copy in pages:
        copy.wait()


def line_kernel(b0, b1, b2, b3, line_ref):
    for at, block in enumerate((b0, b1, b2, b3)):
        line_ref[at] = block[...]


def relay_kernel(*refs):
    *parts, _, out_ref = refs
    at = 0
    for part in parts:
        out_ref[at : at + part.shape[0]] = part[...]
        at += part.shape[0]


def relay(*parts, tie):
    length = sum(part.shape[0] for part in parts)
    return pl.pallas_call(
        relay_kernel,
        out_shape=jax.ShapeDtypeStruct((length,) + parts[0].shape[1:], parts[0].dtype),
        in_specs=[VMEM] * len(parts) + [ANY],
        out_specs=VMEM,
        compiler_params=pltpu.CompilerParams(vmem_limit_bytes=4 << 20),
        name="relay",
    )(*parts, tie)


def by_groups(count, group, copies, work):
    group = math.gcd(count, group)

    @pl.loop(0, count // group)
    def _(at):
        experts = [at * group + e for e in range(group)]
        for e in experts:
            for copy in copies(e):
                copy.wait()
        work(experts)


def up_kernel(pieces, here, *refs):
    first, last = pieces[0] == 0, pieces[-1] == 3
    count = len(pieces)
    if not first:
        line = refs[0].shape[0] // 2
        blocks = [ref.at[pl.ds(at, line)] for ref in refs[:count] for at in (0, line)]
        refs = refs[count:]
    else:
        blocks, refs = refs[: 2 * count], refs[2 * count :]
    wg_ref, wu_ref = refs[:2]
    refs = refs[2:]
    if first:
        gate_ref, upper_ref, square_ref, hot_ref, share_ref = refs[-10:-5]
        weights, rows, picked, info, sems = refs[-5:]
    elif last:
        gate_in, upper_in, square_in, hot_ref, share_ref = refs[:5]
        hid_ref, weights, rows, picked, info, sems, inverse = refs[-7:]
    else:
        gate_in, upper_in, square_in, hot_ref = refs[:4]
        gate_ref, upper_ref, square_ref, weights, rows, picked, info, sems = refs[-8:]
    line, tall, width = blocks[0].shape
    ranks = 2 * line
    shard_count, _, units = wg_ref.shape
    slab = ranks * CAPACITY
    picks = shard_count * slab
    lanes = ranks * SLAB
    rank, base = here[0], here[2]

    def copies(e):
        for at, piece in enumerate(pieces):
            source = pl.ds(pl.multiple_of((here[1] ^ piece) * width, width), width)
            target = pl.ds(at * width, width)
            for side, ref in enumerate((wg_ref, wu_ref)):
                yield pltpu.make_async_copy(
                    ref.at[e, source], weights.at[e, side, target], sems.at[2 * at + side, e]
                )

    @pl.loop(0, shard_count)
    def _(e):
        for copy in copies(e):
            copy.start()

    @pl.loop(0, line)
    def _(m):
        for at, ref in enumerate(blocks):
            at, side = at // 2, at % 2
            dp = rank ^ (2 * m + side)
            to = pl.ds(pl.multiple_of(dp * SLAB, SLAB), SLAB)
            values = ref[m].astype(F32)
            for step in range(STEPS):
                rows[step, to, pl.ds(at * width, width)] = values[
                    step * 12 : step * 12 + SLAB
                ].astype(BF16)
            info[at, dp] = values[tall - 8 :, : 4 * LANES]

    slot_at = lax.broadcasted_iota(jnp.int32, (4, lanes), 1) // SLAB

    def line_of(at, number):
        group = pl.ds(number // PIECES * LANES, LANES)
        found = jnp.zeros((4, lanes), F32)
        for d in range(ranks):
            found += jnp.where(slot_at == (number + d) % PIECES, info[at, d, 4:, group], 0.0)
        back = number % PIECES * SLAB
        return pltpu.roll(found, lanes - back, 1) if back else found

    squares = []
    for step in range(STEPS):
        total = sum(line_of(at, 18 + 3 * step + part) for at in range(count) for part in range(3))
        squares.append(total[:1] if first else total[:1] + square_in[step : step + 1])
        if not last:
            square_ref[pl.ds(step, 1), :] = squares[step]
    if first:
        row_at = lax.broadcasted_iota(jnp.int32, (picks, lanes), 0)
        lane_at = lax.broadcasted_iota(jnp.int32, (picks, lanes), 1)
        owner = (row_at % slab) // CAPACITY
        wanted = (base + row_at // slab) * CAPACITY + row_at % CAPACITY + 1
        wanted = jnp.where(lane_at // SLAB == owner, wanted, -1).astype(F32)
        for step in range(STEPS):
            hot = jnp.zeros((picks, lanes), F32)
            gate = jnp.zeros((picks, lanes), F32)
            for side in range(2):
                number = (2 * step + side) * 3
                marks = line_of(0, number)
                share = line_of(0, number + 1) + line_of(0, number + 2)
                for k in range(4):
                    found = marks[k : k + 1] == wanted
                    hot = jnp.where(found, 1.0, hot)
                    gate = jnp.where(found, share[k : k + 1], gate)
            hot_ref[step] = hot.astype(BF16)
            gate = jnp.broadcast_to(jnp.sum(gate, axis=-1, keepdims=True), (picks, units))
            share_ref[:, pl.ds(step * slab, slab), :] = gate.reshape(shard_count, slab, units)

    for step in range(STEPS):
        hot = hot_ref[step]
        for n in range(0, count * width, 256):
            for half in range(0, picks, picks // 2):
                chosen = jnp.dot(
                    hot[half : half + picks // 2],
                    rows[step, :, n : n + 256],
                    preferred_element_type=F32,
                ).astype(BF16)
                picked[
                    pl.ds(half // slab, shard_count // 2), pl.ds(step * slab, slab), pl.ds(n, 256)
                ] = chosen.reshape(shard_count // 2, slab, 256)
        if last:
            found = hot.astype(F32) * lax.rsqrt(squares[step] / D + EPS)
            found = jnp.broadcast_to(jnp.sum(found, axis=-1, keepdims=True), (picks, units))
            inverse[:, pl.ds(step * slab, slab), :] = found.reshape(shard_count, slab, units)

    def multiply(experts):
        gates = [jnp.dot(picked[e], weights[e, 0], preferred_element_type=F32) for e in experts]
        uppers = [jnp.dot(picked[e], weights[e, 1], preferred_element_type=F32) for e in experts]
        for e, gate, upper in zip(experts, gates, uppers):
            if not first:
                gate = gate + gate_in[e]
                upper = upper + upper_in[e]
            if last:
                gate = gate * inverse[e]
                upper = upper * inverse[e]
                hid_ref[e] = (gate * jax.nn.sigmoid(gate) * upper * share_ref[e]).astype(BF16)
            else:
                gate_ref[e] = gate
                upper_ref[e] = upper

    by_groups(shard_count, 2, copies, multiply)


def up_pieces(pieces, here, blocks, w_gate, w_up, so_far=(), ties=()):
    width = blocks[0].shape[2]
    shard_count, _, units = w_gate.shape
    ranks = lax.axis_size("dp")
    slab = ranks * CAPACITY
    depth = len(pieces) * width
    product = jax.ShapeDtypeStruct((shard_count, STEPS * slab, units), F32)
    hidden = jax.ShapeDtypeStruct(product.shape, BF16)
    square = jax.ShapeDtypeStruct((STEPS, LANES), F32)
    hot = jax.ShapeDtypeStruct((STEPS, shard_count * slab, ranks * SLAB), BF16)
    out = [product, product, square]
    if pieces[0] == 0:
        out += [hot, product]
    if pieces[-1] == 3:
        out = [hidden]
    scratch = [
        pltpu.VMEM((shard_count, 2, depth, units), BF16),
        pltpu.VMEM((STEPS, ranks * SLAB, depth), BF16),
        pltpu.VMEM((shard_count, STEPS * slab, depth), BF16),
        pltpu.VMEM((len(pieces), ranks, 8, 4 * LANES), F32),
        pltpu.SemaphoreType.DMA((2 * len(pieces), shard_count)),
    ]
    if pieces[-1] == 3:
        scratch.append(pltpu.VMEM(product.shape, F32))
    return pl.pallas_call(
        functools.partial(up_kernel, pieces),
        out_shape=out,
        in_specs=[SMEM] + [VMEM] * len(blocks) + [ANY] * 2 + [VMEM] * len(so_far) + [ANY] * len(ties),
        out_specs=[VMEM] * len(out),
        scratch_shapes=scratch,
        compiler_params=pltpu.CompilerParams(vmem_limit_bytes=32 << 20),
        cost_estimate=pl.CostEstimate(
            flops=1_000_000, bytes_accessed=len(pieces) * 100_000, transcendentals=1000
        ),
        name="gate_and_up",
    )(here, *blocks, w_gate, w_up, *so_far, *ties)


def down_kernel(piece, here, own_ref, other_ref, hot_ref, w_ref, *refs):
    weights, hidden, made, sums, sems = refs[-5:]
    if piece == 0:
        out_ref = refs[-6]
    else:
        out_ref, send_ref = refs[-7:-5]
    shard_count, _, units = own_ref.shape
    width = w_ref.shape[2]
    slab = made.shape[1] // shard_count
    rep = here[1]
    part = pl.ds(pl.multiple_of(((rep >> 1) ^ piece) * 2 * units, 2 * units), 2 * units)

    def copies(e):
        return [pltpu.make_async_copy(w_ref.at[e, part], weights.at[e], sems.at[e])]

    @pl.loop(0, shard_count)
    def _(e):
        copies(e)[0].start()

    for at, ref in enumerate((own_ref, other_ref)):
        at = ((rep & 1) ^ at) * units
        hidden[:, :, pl.ds(pl.multiple_of(at, units), units)] = ref[...]

    def multiply(experts):
        for e in experts:
            output = jnp.dot(hidden[e], weights[e], preferred_element_type=F32).astype(BF16)
            for step in range(STEPS):
                made[step, pl.ds(pl.multiple_of(e * slab, slab), slab), :] = output[
                    step * slab : (step + 1) * slab
                ]

    by_groups(shard_count, 4, copies, multiply)
    contract = (((0,), (0,)), ((), ()))
    for n in range(0, width, 256):
        at = slice(n, n + 256)
        for step in range(STEPS):
            total = lax.dot_general(
                hot_ref[step], made[step, :, at], contract, preferred_element_type=F32
            )
            if piece == 0:
                out_ref[step, :, at] = total
            else:
                sums[step, :, at] = refs[0][step, :, at] + total
    if piece == 1:
        for side, ref in enumerate((out_ref, send_ref)):
            for z in range(out_ref.shape[0]):
                at = pl.ds(pl.multiple_of((2 * z + ((here[0] & 1) ^ side)) * SLAB, SLAB), SLAB)
                ref[z] = jnp.concatenate(
                    [
                        sums[step, at, n : n + LANES][:12]
                        for step in range(STEPS)
                        for n in range(0, width, LANES)
                    ],
                    axis=0,
                ).astype(BF16)


def down_piece(piece, here, own, other, hot, w_down, so_far=(), ties=()):
    shard_count, _, width = w_down.shape
    _, picks, lanes = hot.shape
    units = own.shape[2]
    if piece == 0:
        out = [jax.ShapeDtypeStruct((STEPS, lanes, width), F32)]
    else:
        half = (lanes // SLAB // 2, STEPS * 12 * width // LANES, LANES)
        out = [jax.ShapeDtypeStruct(half, BF16)] * 2
    return pl.pallas_call(
        functools.partial(down_kernel, piece),
        out_shape=out,
        in_specs=[SMEM] + [VMEM] * 3 + [ANY] + [VMEM] * len(so_far) + [ANY] * len(ties),
        out_specs=[VMEM] * len(out),
        scratch_shapes=[
            pltpu.VMEM((shard_count, 2 * units, width), BF16),
            pltpu.VMEM((shard_count, own.shape[1], 2 * units), BF16),
            pltpu.VMEM((STEPS, picks, width), BF16),
            pltpu.VMEM((STEPS, lanes, width), F32),
            pltpu.SemaphoreType.DMA((shard_count,)),
        ],
        compiler_params=pltpu.CompilerParams(vmem_limit_bytes=24 << 20),
        cost_estimate=pl.CostEstimate(
            flops=1_000_000, bytes_accessed=100_000, transcendentals=0
        ),
        name="down",
    )(here, own, other, hot, w_down, *so_far, *ties)


def fold_kernel(here, keep_ref, got_ref, tie, own_ref, *send_refs):
    z = here[0] // 2
    own_ref[...] = keep_ref[z].astype(F32) + got_ref[z].astype(F32)
    for at, ref in enumerate(send_refs):
        to = z ^ (at + 1)
        ref[...] = (keep_ref[to].astype(F32) + got_ref[to].astype(F32)).astype(BF16)


def finish_kernel(own_ref, *refs):
    *parts, out_ref = refs
    total = own_ref[...]
    for part in parts:
        total = total + part[...].astype(F32)
    row_count = out_ref.shape[1]
    at = 0
    for step in range(STEPS):
        for n in range(0, out_ref.shape[2], LANES):
            out_ref[step, :, n : n + LANES] = total[at : at + row_count].astype(BF16)
            at += row_count


def gathered(
    q_raw, k_raw, v_raw, q_gain, k_gain, kv_pool, page_table, cache_len, out_pages, in_slots,
    hidden_in, ln_gain, route_ids, route_logits, w_gate, w_up, w_down,
):
    ranks = lax.axis_size("dp")
    shard_count = w_gate.shape[0]
    row_count = hidden_in.shape[1]
    width = hidden_in.shape[2]
    tall = STEPS * row_count + 4
    rank = lax.axis_index("dp").astype(jnp.int32)
    rep = lax.axis_index("rep").astype(jnp.int32)
    here = jnp.stack([rank, rep, rank * shard_count % EXPERTS])
    pool = kv_pool.reshape(kv_pool.shape[0], -1, kv_pool.shape[3])
    small = pltpu.CompilerParams(vmem_limit_bytes=4 << 20)
    ids = route_ids.transpose(0, 2, 1)
    logits = route_logits.transpose(0, 2, 1)
    block, leaving = pl.pallas_call(
        block_kernel,
        out_shape=(
            jax.ShapeDtypeStruct((tall, width), BF16),
            jax.ShapeDtypeStruct(out_pages.shape + pool.shape[1:], BF16),
        ),
        in_specs=[SMEM] + [ANY] * 6,
        out_specs=(VMEM, ANY),
        scratch_shapes=[
            pltpu.VMEM(ids.shape, jnp.int32),
            pltpu.VMEM(logits.shape, F32),
            pltpu.VMEM(hidden_in.shape, BF16),
            pltpu.VMEM((1, width), F32),
            pltpu.SMEM(out_pages.shape, jnp.int32),
            pltpu.VMEM((STEPS, 2, TOP_K, LANES), F32),
            pltpu.SemaphoreType.DMA((5,)),
            pltpu.SemaphoreType.DMA(out_pages.shape),
        ],
        compiler_params=small,
        name="token_block",
    )(
        here, in_hbm(out_pages), in_hbm(ids), in_hbm(logits), in_hbm(hidden_in), in_hbm(ln_gain[None]),
        in_hbm(pool),
    )
    w_gate, w_up, w_down = in_hbm(w_gate), in_hbm(w_up), in_hbm(w_down)
    own = pl.pallas_call(
        line_kernel,
        out_shape=jax.ShapeDtypeStruct((ranks // 2, tall, width), BF16),
        in_specs=[VMEM] * 4,
        out_specs=VMEM,
        compiler_params=small,
        name="line",
    )(block, *[swap(block, "dp", bits) for bits in (2, 4, 6)])
    other = swap(own, "dp", 1)
    far_own = swap(own, "rep", 2)
    near_own = swap(own, "rep", 1)
    arriving = lax.ppermute(leaving, "dp", [(i, (i + ranks // 2) % ranks) for i in range(ranks)])
    far_other = swap(other, "rep", 2)
    near_other = swap(other, "rep", 1)
    *sums, hot, share = up_pieces(
        (0, 1), here, (own, other, near_own, near_other), w_gate, w_up, ties=(far_own,)
    )
    far = relay(far_own, far_other, tie=sums[2])
    last = swap(far, "rep", 1)
    (hidden,) = up_pieces((2, 3), here, (far, last), w_gate, w_up, (*sums, hot, share))
    near = swap(hidden, "rep", 1)
    far = swap(hidden, "rep", 2)
    (sums,) = down_piece(0, here, hidden, near, hot, w_down, ties=(arriving,))
    far = relay(far, tie=sums)
    last = swap(far, "rep", 1)
    keep, send = down_piece(1, here, far, last, hot, w_down, (sums,))
    got = swap(send, "dp", 1)
    attend = functools.partial(
        attention, arriving, q_raw, k_raw, v_raw, q_gain, k_gain, pool, page_table, cache_len, in_slots
    )
    beside_y = row_count * 3 // 4
    attn_out = attend(0, beside_y, tie=keep)
    part = jax.ShapeDtypeStruct(keep.shape[1:], BF16)
    own, *sends = pl.pallas_call(
        fold_kernel,
        out_shape=[jax.ShapeDtypeStruct(part.shape, F32)] + [part] * 3,
        in_specs=[SMEM] + [VMEM] * 2 + [ANY],
        out_specs=[VMEM] * 4,
        compiler_params=small,
        name="fold",
    )(here, keep, got, attn_out)
    parts = [swap(send, "dp", 2 * at + 2) for at, send in enumerate(sends)]
    attn_out = attend(beside_y, row_count - beside_y, attn_out, tie=own)
    moe_out = pl.pallas_call(
        finish_kernel,
        out_shape=jax.ShapeDtypeStruct(hidden_in.shape, BF16),
        in_specs=[VMEM] * 4,
        out_specs=VMEM,
        compiler_params=small,
        name="finish",
    )(own, *parts)
    return attn_out, moe_out


def experts_exchanged(hidden_in, ln_gain, route_ids, route_logits, w_gate, w_up, w_down):
    ranks = lax.axis_size("dp")
    row_count = hidden_in.shape[1]
    whole_rows = lax.all_gather(hidden_in, "rep", axis=2, tiled=True)
    values = whole_rows.astype(F32)
    mean_square = jnp.mean(values * values, axis=-1, keepdims=True)
    normed = (values * lax.rsqrt(mean_square + EPS) * ln_gain).astype(BF16)
    slots = place(route_ids)
    targets = route_ids * CAPACITY + slots
    expert_slots = jnp.arange(EXPERTS * CAPACITY, dtype=jnp.int32)
    hits = jnp.any(targets[:, None, :, :] == expert_slots[None, :, None, None], axis=-1)
    hits = hits.astype(BF16).reshape(STEPS, EXPERTS, CAPACITY, row_count)
    packed = jnp.einsum("secr,srd->escd", hits, normed, preferred_element_type=F32).astype(BF16)
    outgoing = jnp.broadcast_to(packed[None], (2,) + packed.shape).reshape(
        ranks, -1, packed.shape[-1]
    )
    incoming = lax.all_to_all(outgoing, "dp", split_axis=0, concat_axis=0, tiled=True)
    local_count = w_gate.shape[0]
    arrived = incoming.reshape(ranks, local_count, STEPS * CAPACITY, D)
    gate = jnp.einsum("nlrd,ldf->nlrf", arrived, w_gate, preferred_element_type=F32)
    upper = jnp.einsum("nlrd,ldf->nlrf", arrived, w_up, preferred_element_type=F32)
    hidden_part = (jax.nn.silu(gate) * upper).astype(BF16)
    hidden_all = lax.all_gather(hidden_part, "rep", axis=3, tiled=True)
    produced = jnp.einsum("nlrf,lfd->nlrd", hidden_all, w_down, preferred_element_type=F32)
    produced = produced.astype(BF16)
    returned = lax.all_to_all(
        produced.reshape(ranks, -1, produced.shape[-1]), "dp", split_axis=0, concat_axis=0, tiled=True
    )
    returned = returned.reshape(2, EXPERTS, STEPS, CAPACITY, -1).astype(F32)
    both_halves = returned[0] + returned[1]
    section_index = jnp.broadcast_to(
        jnp.arange(STEPS, dtype=jnp.int32)[:, None, None], route_ids.shape
    )
    picked = both_halves[route_ids, section_index, slots]
    weights = jax.nn.softmax(route_logits, axis=-1)
    return jnp.sum(weights[..., None] * picked, axis=2).astype(BF16)


def exchanged(
    q_raw, k_raw, v_raw, q_gain, k_gain, kv_pool, page_table, cache_len, out_pages, in_slots,
    hidden_in, ln_gain, route_ids, route_logits, w_gate, w_up, w_down,
):
    ranks = lax.axis_size("dp")
    pool = kv_pool.reshape(kv_pool.shape[0], -1, kv_pool.shape[3])
    leaving = pool[out_pages]
    arriving = lax.ppermute(leaving, "dp", [(i, (i + ranks // 2) % ranks) for i in range(ranks)])
    attn_out = attention(
        arriving, q_raw, k_raw, v_raw, q_gain, k_gain, pool, page_table, cache_len, in_slots,
        0, q_raw.shape[1],
    )
    moe_out = experts_exchanged(hidden_in, ln_gain, route_ids, route_logits, w_gate, w_up, w_down)
    return attn_out, moe_out


def local(*args):
    plan = gathered if (lax.axis_size("dp"), lax.axis_size("rep")) == (8, 4) else exchanged
    return plan(*args)


def solution(mesh):
    return jax.shard_map(
        local,
        mesh=mesh,
        in_specs=(
            P(None, "dp", "rep"),
            P(None, "dp", "rep"),
            P(None, "dp", "rep"),
            P(),
            P(),
            P("dp", None, None, "rep"),
            P("dp", None),
            P("dp"),
            P("dp"),
            P("dp"),
            P(None, "dp", "rep"),
            P(),
            P(None, "dp", None),
            P(None, "dp", None),
            P("dp", None, "rep"),
            P("dp", None, "rep"),
            P("dp", None, "rep"),
        ),
        out_specs=(P(None, "dp", "rep"), P(None, "dp", "rep")),
        check_vma=False,
    )
```

```python
import functools
import math

import jax
import jax.numpy as jnp
import numpy as np
from jax import lax
from jax.experimental import pallas as pl
from jax.experimental.pallas import tpu as pltpu
from jax.sharding import PartitionSpec as P

D = 4096
HEAD_DIM = 128
EXPERTS = 64
STEPS = 3
CAPACITY = 2
TOP_K = 8
SLAB = 16
LANES = 128
PIECES = LANES // SLAB

EPS = 1e-06
THETA = 1000000.0

BF16 = jnp.bfloat16
F32 = jnp.float32
ANY = pl.BlockSpec(memory_space=pl.ANY)
VMEM = pl.BlockSpec(memory_space=pltpu.VMEM)
SMEM = pl.BlockSpec(memory_space=pltpu.SMEM)


def place(route_ids):
    flat_ids = route_ids.reshape(route_ids.shape[0], -1)
    hot_table = (
        flat_ids[:, :, None] == jnp.arange(EXPERTS, dtype=jnp.int32)[None, None, :]
    ).astype(jnp.int32)
    before = jnp.cumsum(hot_table, axis=1) - hot_table
    return jnp.sum(before * hot_table, axis=2).reshape(route_ids.shape)


def attention_kernel(
    first, count, table, lengths, slots_in, q_ref, k_ref, v_ref, qg_ref, kg_ref, speed_ref, pool_ref, new_ref, *refs
):
    out_ref, source, angles = refs[-3:]
    pool_count = pool_ref.shape[0]
    new_count = new_ref.shape[0]
    row_count = q_ref.shape[1]
    page_count = table.shape[0]
    page_rows = pool_ref.shape[1]
    heads = q_ref.shape[2] // HEAD_DIM
    if first:
        out_ref[...] = refs[0][...]
    for slot in range(pool_count):
        source[slot] = -1
    for at in range(new_count):
        source[slots_in[at]] = at

    def page_of(slot):
        at = source[slot]
        return jnp.where(at >= 0, new_ref[jnp.maximum(at, 0)], pool_ref[slot])

    scaling = 1.0 / math.sqrt(HEAD_DIM)
    angles[...] = jnp.zeros(angles.shape, F32)
    for step in range(STEPS):
        for row in range(row_count):
            position = (lengths[row] + step).astype(F32)
            angles[pl.ds(step * row_count + row, 1), :] = speed_ref[...] * position
    first_half = lax.broadcasted_iota(jnp.int32, angles.shape, 1) < HEAD_DIM // 2
    cosines = jnp.cos(angles[...])
    sines = jnp.sin(angles[...])
    sines = jnp.where(first_half, -sines, sines)

    def turned(values, gain, cosine, sine):
        mean_square = jnp.mean(values * values, axis=-1, keepdims=True)
        normed = values * lax.rsqrt(mean_square + EPS) * gain
        return (normed * cosine + pltpu.roll(normed, HEAD_DIM // 2, 1) * sine).astype(BF16)

    width = page_count * page_rows
    column = lax.broadcasted_iota(jnp.int32, (STEPS * heads, width), 1)
    fresh_column = lax.broadcasted_iota(jnp.int32, (STEPS * heads, STEPS), 1)
    fresh_row = lax.broadcasted_iota(jnp.int32, (STEPS * heads, STEPS), 0) // heads
    for row in range(first, first + count):
        queries = []
        keys = []
        for step in range(STEPS):
            at = step * row_count + row
            cosine = cosines[at : at + 1]
            sine = sines[at : at + 1]
            raw = q_ref[step, pl.ds(row, 1), :].astype(F32)
            raw = jnp.concatenate(
                [raw[:, h * HEAD_DIM : (h + 1) * HEAD_DIM] for h in range(heads)], axis=0
            )
            queries.append(turned(raw, qg_ref[...], cosine, sine))
            keys.append(turned(k_ref[step, pl.ds(row, 1), :].astype(F32), kg_ref[...], cosine, sine))
        queries = jnp.concatenate(queries, axis=0)
        context = jnp.concatenate(
            [page_of(table[page, row]) for page in range(page_count)], axis=0
        )
        contract = (((1,), (1,)), ((), ()))
        scores = lax.dot_general(queries, context, contract, preferred_element_type=F32) * scaling
        valid = (column < 2 * lengths[row]) & (column % 2 == 0)
        scores = jnp.where(valid, scores, -1e30)
        fresh = jnp.concatenate(
            [
                jnp.sum(queries.astype(F32) * key.astype(F32), axis=-1, keepdims=True)
                for key in keys
            ],
            axis=1,
        )
        fresh = jnp.where(fresh_column <= fresh_row, fresh * scaling, -1e30)
        top = jnp.maximum(
            jnp.max(scores, axis=-1, keepdims=True), jnp.max(fresh, axis=-1, keepdims=True)
        )
        expos = jnp.where(valid, jnp.exp(scores - top), 0.0)
        fresh = jnp.where(fresh_column <= fresh_row, jnp.exp(fresh - top), 0.0)
        total = jnp.sum(expos, axis=-1, keepdims=True) + jnp.sum(fresh, axis=-1, keepdims=True)
        probs = pltpu.roll(expos / total, 1, 1).astype(BF16)
        mixed = jnp.dot(probs, context, preferred_element_type=F32)
        fresh = (fresh / total).astype(BF16).astype(F32)
        for step in range(STEPS):
            value = v_ref[step, pl.ds(row, 1), :].astype(F32)
            mixed = mixed + fresh[:, step : step + 1] * value
        for step in range(STEPS):
            part = mixed[step * heads : (step + 1) * heads]
            out_ref[step, pl.ds(row, 1), :] = jnp.concatenate(
                [part[h : h + 1] for h in range(heads)], axis=1
            ).astype(BF16)


def attention(
    arriving, q_raw, k_raw, v_raw, q_gain, k_gain, pool, page_table, cache_len, in_slots, first, count,
    so_far=None, tie=None
):
    extra = [x for x in (so_far, tie) if x is not None]
    row_count = q_raw.shape[1]
    exponent = np.arange(HEAD_DIM // 2, dtype=np.float32) * np.float32(2.0 / HEAD_DIM)
    speed = np.power(np.float32(THETA), -exponent)
    speed = jnp.asarray(np.concatenate([speed, speed])[None], F32)
    scratch = [
        pltpu.SMEM((pool.shape[0],), jnp.int32),
        pltpu.VMEM((-(-STEPS * row_count // 8) * 8, HEAD_DIM), F32),
    ]
    return pl.pallas_call(
        functools.partial(attention_kernel, first, count),
        out_shape=jax.ShapeDtypeStruct(q_raw.shape, BF16),
        in_specs=[SMEM] * 3 + [VMEM] * (8 + (so_far is not None)) + [ANY] * (tie is not None),
        out_specs=VMEM,
        scratch_shapes=scratch,
        compiler_params=pltpu.CompilerParams(vmem_limit_bytes=12 << 20),
        cost_estimate=pl.CostEstimate(
            flops=400_000_000, bytes_accessed=8_000_000, transcendentals=400_000
        ),
        name="attention",
    )(
        page_table.T, cache_len, in_slots, q_raw, k_raw, v_raw, q_gain[None], k_gain[None], speed,
        pool, arriving, *extra,
    )


def swap(x, axis, bits):
    size = lax.axis_size(axis)
    return lax.ppermute(x, axis, [(i, i ^ bits) for i in range(size)])


def in_hbm(x):
    return pltpu.with_memory_space_constraint(x, pltpu.HBM)


def block_kernel(
    here, out_pages, ids_hbm, logits_hbm, hidden_hbm, gain_hbm, pool_ref, out_ref, leaving, ids_ref,
    logits_ref, hidden_ref, gain_ref, page_ids, wide, sems, page_sems,
):
    rank = here[0]
    row_count = ids_ref.shape[2]
    width = out_ref.shape[1]
    part = pl.ds(pl.multiple_of(here[1] * width, width), width)
    copies = [
        pltpu.make_async_copy(source, target, sems.at[at])
        for at, (source, target) in enumerate(
            (
                (ids_hbm, ids_ref),
                (logits_hbm, logits_ref),
                (hidden_hbm, hidden_ref),
                (gain_hbm.at[:, part], gain_ref),
                (out_pages, page_ids),
            )
        )
    ]
    for copy in copies:
        copy.start()
    lane_at = lax.broadcasted_iota(jnp.int32, (TOP_K, LANES), 1)
    wide[...] = jnp.zeros(wide.shape, F32)
    copies[4].wait()
    pages = [
        pltpu.make_async_copy(pool_ref.at[page_ids[at]], leaving.at[at], page_sems.at[at])
        for at in range(leaving.shape[0])
    ]
    for copy in pages:
        copy.start()
    copies[0].wait()
    copies[1].wait()
    groups = [jnp.zeros((4, LANES), F32) for _ in range(4)]

    def put(piece, value):
        turned = pltpu.roll(value, ((piece + rank) % PIECES) * SLAB, 1)
        groups[piece // PIECES] += turned

    for step in range(STEPS):
        wide[step, 0, :, :row_count] = ids_ref[step].astype(F32)
        wide[step, 1, :, :row_count] = logits_ref[step]
        ids = wide[step, 0]
        logits = wide[step, 1]
        expos = jnp.exp(logits - jnp.max(logits, axis=0, keepdims=True))
        weights = expos / jnp.sum(expos, axis=0, keepdims=True)
        high = weights.astype(BF16).astype(F32)
        slot = jnp.zeros((TOP_K, LANES), F32)
        for back in range(1, row_count):
            earlier = pltpu.roll(ids, back, 1)
            for k in range(TOP_K):
                same = (ids == earlier[k : k + 1]) & (lane_at >= back)
                slot = slot + jnp.where(same, 1.0, 0.0)
        for at, value in enumerate((ids * CAPACITY + slot + 1.0, high, weights - high)):
            value = jnp.where(lane_at < row_count, value, 0.0)
            for side in range(2):
                put((2 * step + side) * 3 + at, value[4 * side : 4 * side + 4])
    copies[2].wait()
    copies[3].wait()
    gain = gain_ref[...]
    row_at = lax.broadcasted_iota(jnp.int32, (row_count, LANES), 0)
    column_at = lax.broadcasted_iota(jnp.int32, (row_count, LANES), 1)
    rows = []
    for step in range(STEPS):
        values = hidden_ref[step].astype(F32)
        square = jnp.sum(values * values, axis=-1, keepdims=True)
        rest = jnp.sum(jnp.where(row_at == column_at, square, 0.0), axis=0, keepdims=True)
        rest = jnp.concatenate([rest, jnp.zeros((3, LANES), F32)], axis=0)
        for at in range(3):
            high = rest.astype(BF16).astype(F32)
            put(18 + 3 * step + at, high)
            rest = rest - high
        rows.append(values * gain)
    groups.append(jnp.zeros((4, width - 4 * LANES), F32))
    out_ref[...] = jnp.concatenate(rows + [jnp.concatenate(groups, axis=1)], axis=0).astype(BF16)
    for copy in pages:
        copy.wait()


def line_kernel(b0, b1, b2, b3, line_ref):
    for at, block in enumerate((b0, b1, b2, b3)):
        line_ref[at] = block[...]


def relay_kernel(*refs):
    *parts, _, out_ref = refs
    at = 0
    for part in parts:
        out_ref[at : at + part.shape[0]] = part[...]
        at += part.shape[0]


def relay(*parts, tie):
    length = sum(part.shape[0] for part in parts)
    return pl.pallas_call(
        relay_kernel,
        out_shape=jax.ShapeDtypeStruct((length,) + parts[0].shape[1:], parts[0].dtype),
        in_specs=[VMEM] * len(parts) + [ANY],
        out_specs=VMEM,
        compiler_params=pltpu.CompilerParams(vmem_limit_bytes=4 << 20),
        name="relay",
    )(*parts, tie)


def by_groups(count, group, copies, work):
    group = math.gcd(count, group)

    @pl.loop(0, count // group)
    def _(at):
        experts = [at * group + e for e in range(group)]
        for e in experts:
            for copy in copies(e):
                copy.wait()
        work(experts)


def up_kernel(pieces, here, *refs):
    first, last = pieces[0] == 0, pieces[-1] == 3
    count = len(pieces)
    if not first:
        line = refs[0].shape[0] // 2
        blocks, refs = [refs[0].at[pl.ds(at, line)] for at in (0, line)], refs[1:]
    else:
        blocks, refs = refs[: 2 * count], refs[2 * count :]
    wg_ref, wu_ref = refs[:2]
    refs = refs[2:]
    if first:
        gate_ref, upper_ref, square_ref, hot_ref, share_ref = refs[-10:-5]
        weights, rows, picked, info, sems = refs[-5:]
    elif last:
        gate_in, upper_in, square_in, hot_ref, share_ref = refs[:5]
        hid_ref, weights, rows, picked, info, sems, inverse = refs[-7:]
    else:
        gate_in, upper_in, square_in, hot_ref = refs[:4]
        gate_ref, upper_ref, square_ref, weights, rows, picked, info, sems = refs[-8:]
    line, tall, width = blocks[0].shape
    ranks = 2 * line
    shard_count, _, units = wg_ref.shape
    slab = ranks * CAPACITY
    picks = shard_count * slab
    lanes = ranks * SLAB
    rank, base = here[0], here[2]

    def copies(e):
        for at, piece in enumerate(pieces):
            source = pl.ds(pl.multiple_of((here[1] ^ piece) * width, width), width)
            target = pl.ds(at * width, width)
            for side, ref in enumerate((wg_ref, wu_ref)):
                yield pltpu.make_async_copy(
                    ref.at[e, source], weights.at[e, side, target], sems.at[2 * at + side, e]
                )

    @pl.loop(0, shard_count)
    def _(e):
        for copy in copies(e):
            copy.start()

    @pl.loop(0, line)
    def _(m):
        for at, ref in enumerate(blocks):
            at, side = at // 2, at % 2
            dp = rank ^ (2 * m + side)
            to = pl.ds(pl.multiple_of(dp * SLAB, SLAB), SLAB)
            values = ref[m].astype(F32)
            for step in range(STEPS):
                rows[step, to, pl.ds(at * width, width)] = values[
                    step * 12 : step * 12 + SLAB
                ].astype(BF16)
            info[at, dp] = values[tall - 8 :, : 4 * LANES]

    slot_at = lax.broadcasted_iota(jnp.int32, (4, lanes), 1) // SLAB

    def line_of(at, number):
        group = pl.ds(number // PIECES * LANES, LANES)
        found = jnp.zeros((4, lanes), F32)
        for d in range(ranks):
            found += jnp.where(slot_at == (number + d) % PIECES, info[at, d, 4:, group], 0.0)
        back = number % PIECES * SLAB
        return pltpu.roll(found, lanes - back, 1) if back else found

    squares = []
    for step in range(STEPS):
        total = sum(line_of(at, 18 + 3 * step + part) for at in range(count) for part in range(3))
        squares.append(total[:1] if first else total[:1] + square_in[step : step + 1])
        if not last:
            square_ref[pl.ds(step, 1), :] = squares[step]
    if first:
        row_at = lax.broadcasted_iota(jnp.int32, (picks, lanes), 0)
        lane_at = lax.broadcasted_iota(jnp.int32, (picks, lanes), 1)
        owner = (row_at % slab) // CAPACITY
        wanted = (base + row_at // slab) * CAPACITY + row_at % CAPACITY + 1
        wanted = jnp.where(lane_at // SLAB == owner, wanted, -1).astype(F32)
        for step in range(STEPS):
            hot = jnp.zeros((picks, lanes), F32)
            gate = jnp.zeros((picks, lanes), F32)
            for side in range(2):
                number = (2 * step + side) * 3
                marks = line_of(0, number)
                share = line_of(0, number + 1) + line_of(0, number + 2)
                for k in range(4):
                    found = marks[k : k + 1] == wanted
                    hot = jnp.where(found, 1.0, hot)
                    gate = jnp.where(found, share[k : k + 1], gate)
            hot_ref[step] = hot.astype(BF16)
            gate = jnp.broadcast_to(jnp.sum(gate, axis=-1, keepdims=True), (picks, units))
            share_ref[:, pl.ds(step * slab, slab), :] = gate.reshape(shard_count, slab, units)

    for step in range(STEPS):
        hot = hot_ref[step]
        for n in range(0, count * width, 256):
            for half in range(0, picks, picks // 2):
                chosen = jnp.dot(
                    hot[half : half + picks // 2],
                    rows[step, :, n : n + 256],
                    preferred_element_type=F32,
                ).astype(BF16)
                picked[
                    pl.ds(half // slab, shard_count // 2), pl.ds(step * slab, slab), pl.ds(n, 256)
                ] = chosen.reshape(shard_count // 2, slab, 256)
        if last:
            found = hot.astype(F32) * lax.rsqrt(squares[step] / D + EPS)
            found = jnp.broadcast_to(jnp.sum(found, axis=-1, keepdims=True), (picks, units))
            inverse[:, pl.ds(step * slab, slab), :] = found.reshape(shard_count, slab, units)

    def multiply(experts):
        gates = [jnp.dot(picked[e], weights[e, 0], preferred_element_type=F32) for e in experts]
        uppers = [jnp.dot(picked[e], weights[e, 1], preferred_element_type=F32) for e in experts]
        for e, gate, upper in zip(experts, gates, uppers):
            if not first:
                gate = gate + gate_in[e]
                upper = upper + upper_in[e]
            if last:
                gate = gate * inverse[e]
                upper = upper * inverse[e]
                hid_ref[e] = (gate * jax.nn.sigmoid(gate) * upper * share_ref[e]).astype(BF16)
            else:
                gate_ref[e] = gate
                upper_ref[e] = upper

    by_groups(shard_count, 4 // count, copies, multiply)


def up_pieces(pieces, here, blocks, w_gate, w_up, so_far=(), ties=()):
    width = blocks[0].shape[2]
    shard_count, _, units = w_gate.shape
    ranks = lax.axis_size("dp")
    slab = ranks * CAPACITY
    depth = len(pieces) * width
    product = jax.ShapeDtypeStruct((shard_count, STEPS * slab, units), F32)
    hidden = jax.ShapeDtypeStruct(product.shape, BF16)
    square = jax.ShapeDtypeStruct((STEPS, LANES), F32)
    hot = jax.ShapeDtypeStruct((STEPS, shard_count * slab, ranks * SLAB), BF16)
    out = [product, product, square]
    if pieces[0] == 0:
        out += [hot, product]
    if pieces[-1] == 3:
        out = [hidden]
    scratch = [
        pltpu.VMEM((shard_count, 2, depth, units), BF16),
        pltpu.VMEM((STEPS, ranks * SLAB, depth), BF16),
        pltpu.VMEM((shard_count, STEPS * slab, depth), BF16),
        pltpu.VMEM((len(pieces), ranks, 8, 4 * LANES), F32),
        pltpu.SemaphoreType.DMA((2 * len(pieces), shard_count)),
    ]
    if pieces[-1] == 3:
        scratch.append(pltpu.VMEM(product.shape, F32))
    return pl.pallas_call(
        functools.partial(up_kernel, pieces),
        out_shape=out,
        in_specs=[SMEM] + [VMEM] * len(blocks) + [ANY] * 2 + [VMEM] * len(so_far) + [ANY] * len(ties),
        out_specs=[VMEM] * len(out),
        scratch_shapes=scratch,
        compiler_params=pltpu.CompilerParams(vmem_limit_bytes=32 << 20),
        cost_estimate=pl.CostEstimate(
            flops=1_000_000, bytes_accessed=len(pieces) * 100_000, transcendentals=1000
        ),
        name="gate_and_up",
    )(here, *blocks, w_gate, w_up, *so_far, *ties)


def down_kernel(piece, here, own_ref, other_ref, hot_ref, w_ref, *refs):
    weights, hidden, made, sums, sems = refs[-5:]
    if piece == 0:
        out_ref = refs[-6]
    else:
        out_ref, send_ref = refs[-7:-5]
    shard_count, _, units = own_ref.shape
    width = w_ref.shape[2]
    slab = made.shape[1] // shard_count
    rep = here[1]
    part = pl.ds(pl.multiple_of(((rep >> 1) ^ piece) * 2 * units, 2 * units), 2 * units)

    def copies(e):
        return [pltpu.make_async_copy(w_ref.at[e, part], weights.at[e], sems.at[e])]

    @pl.loop(0, shard_count)
    def _(e):
        copies(e)[0].start()

    for at, ref in enumerate((own_ref, other_ref)):
        at = ((rep & 1) ^ at) * units
        hidden[:, :, pl.ds(pl.multiple_of(at, units), units)] = ref[...]

    def multiply(experts):
        for e in experts:
            output = jnp.dot(hidden[e], weights[e], preferred_element_type=F32).astype(BF16)
            for step in range(STEPS):
                made[step, pl.ds(pl.multiple_of(e * slab, slab), slab), :] = output[
                    step * slab : (step + 1) * slab
                ]

    by_groups(shard_count, 4, copies, multiply)
    contract = (((0,), (0,)), ((), ()))
    for n in range(0, width, 256):
        at = slice(n, n + 256)
        for step in range(STEPS):
            total = lax.dot_general(
                hot_ref[step], made[step, :, at], contract, preferred_element_type=F32
            )
            if piece == 0:
                out_ref[step, :, at] = total
            else:
                sums[step, :, at] = refs[0][step, :, at] + total
    if piece == 1:
        for side, ref in enumerate((out_ref, send_ref)):
            for z in range(out_ref.shape[0]):
                at = pl.ds(pl.multiple_of((2 * z + ((here[0] & 1) ^ side)) * SLAB, SLAB), SLAB)
                ref[z] = jnp.concatenate(
                    [
                        sums[step, at, n : n + LANES][:12]
                        for step in range(STEPS)
                        for n in range(0, width, LANES)
                    ],
                    axis=0,
                ).astype(BF16)


def down_piece(piece, here, own, other, hot, w_down, so_far=(), ties=()):
    shard_count, _, width = w_down.shape
    _, picks, lanes = hot.shape
    units = own.shape[2]
    if piece == 0:
        out = [jax.ShapeDtypeStruct((STEPS, lanes, width), F32)]
    else:
        half = (lanes // SLAB // 2, STEPS * 12 * width // LANES, LANES)
        out = [jax.ShapeDtypeStruct(half, BF16)] * 2
    return pl.pallas_call(
        functools.partial(down_kernel, piece),
        out_shape=out,
        in_specs=[SMEM] + [VMEM] * 3 + [ANY] + [VMEM] * len(so_far) + [ANY] * len(ties),
        out_specs=[VMEM] * len(out),
        scratch_shapes=[
            pltpu.VMEM((shard_count, 2 * units, width), BF16),
            pltpu.VMEM((shard_count, own.shape[1], 2 * units), BF16),
            pltpu.VMEM((STEPS, picks, width), BF16),
            pltpu.VMEM((STEPS, lanes, width), F32),
            pltpu.SemaphoreType.DMA((shard_count,)),
        ],
        compiler_params=pltpu.CompilerParams(vmem_limit_bytes=24 << 20),
        cost_estimate=pl.CostEstimate(
            flops=1_000_000, bytes_accessed=100_000, transcendentals=0
        ),
        name="down",
    )(here, own, other, hot, w_down, *so_far, *ties)


def fold_kernel(here, keep_ref, got_ref, tie, own_ref, *send_refs):
    z = here[0] // 2
    own_ref[...] = keep_ref[z].astype(F32) + got_ref[z].astype(F32)
    for at, ref in enumerate(send_refs):
        to = z ^ (at + 1)
        ref[...] = (keep_ref[to].astype(F32) + got_ref[to].astype(F32)).astype(BF16)


def finish_kernel(own_ref, *refs):
    *parts, out_ref = refs
    total = own_ref[...]
    for part in parts:
        total = total + part[...].astype(F32)
    row_count = out_ref.shape[1]
    at = 0
    for step in range(STEPS):
        for n in range(0, out_ref.shape[2], LANES):
            out_ref[step, :, n : n + LANES] = total[at : at + row_count].astype(BF16)
            at += row_count


def gathered(
    q_raw, k_raw, v_raw, q_gain, k_gain, kv_pool, page_table, cache_len, out_pages, in_slots,
    hidden_in, ln_gain, route_ids, route_logits, w_gate, w_up, w_down,
):
    ranks = lax.axis_size("dp")
    shard_count = w_gate.shape[0]
    row_count = hidden_in.shape[1]
    width = hidden_in.shape[2]
    tall = STEPS * row_count + 4
    rank = lax.axis_index("dp").astype(jnp.int32)
    rep = lax.axis_index("rep").astype(jnp.int32)
    here = jnp.stack([rank, rep, rank * shard_count % EXPERTS])
    pool = kv_pool.reshape(kv_pool.shape[0], -1, kv_pool.shape[3])
    small = pltpu.CompilerParams(vmem_limit_bytes=4 << 20)
    ids = route_ids.transpose(0, 2, 1)
    logits = route_logits.transpose(0, 2, 1)
    block, leaving = pl.pallas_call(
        block_kernel,
        out_shape=(
            jax.ShapeDtypeStruct((tall, width), BF16),
            jax.ShapeDtypeStruct(out_pages.shape + pool.shape[1:], BF16),
        ),
        in_specs=[SMEM] + [ANY] * 6,
        out_specs=(VMEM, ANY),
        scratch_shapes=[
            pltpu.VMEM(ids.shape, jnp.int32),
            pltpu.VMEM(logits.shape, F32),
            pltpu.VMEM(hidden_in.shape, BF16),
            pltpu.VMEM((1, width), F32),
            pltpu.SMEM(out_pages.shape, jnp.int32),
            pltpu.VMEM((STEPS, 2, TOP_K, LANES), F32),
            pltpu.SemaphoreType.DMA((5,)),
            pltpu.SemaphoreType.DMA(out_pages.shape),
        ],
        compiler_params=small,
        name="token_block",
    )(
        here, in_hbm(out_pages), in_hbm(ids), in_hbm(logits), in_hbm(hidden_in), in_hbm(ln_gain[None]),
        in_hbm(pool),
    )
    w_gate, w_up, w_down = in_hbm(w_gate), in_hbm(w_up), in_hbm(w_down)
    own = pl.pallas_call(
        line_kernel,
        out_shape=jax.ShapeDtypeStruct((ranks // 2, tall, width), BF16),
        in_specs=[VMEM] * 4,
        out_specs=VMEM,
        compiler_params=small,
        name="line",
    )(block, *[swap(block, "dp", bits) for bits in (2, 4, 6)])
    other = swap(own, "dp", 1)
    far_own = swap(own, "rep", 2)
    near_own = swap(own, "rep", 1)
    arriving = lax.ppermute(leaving, "dp", [(i, (i + ranks // 2) % ranks) for i in range(ranks)])
    far_other = swap(other, "rep", 2)
    near_other = swap(other, "rep", 1)
    *sums, hot, share = up_pieces(
        (0, 1), here, (own, other, near_own, near_other), w_gate, w_up, ties=(far_own,)
    )
    far = relay(far_own, far_other, tie=sums[2])
    last = swap(far, "rep", 1)
    sums = up_pieces((2,), here, (far,), w_gate, w_up, (*sums, hot))
    (hidden,) = up_pieces((3,), here, (last,), w_gate, w_up, (*sums, hot, share))
    near = swap(hidden, "rep", 1)
    far = swap(hidden, "rep", 2)
    (sums,) = down_piece(0, here, hidden, near, hot, w_down, ties=(arriving,))
    far = relay(far, tie=sums)
    last = swap(far, "rep", 1)
    keep, send = down_piece(1, here, far, last, hot, w_down, (sums,))
    got = swap(send, "dp", 1)
    attend = functools.partial(
        attention, arriving, q_raw, k_raw, v_raw, q_gain, k_gain, pool, page_table, cache_len, in_slots
    )
    beside_y = row_count * 3 // 4
    attn_out = attend(0, beside_y, tie=keep)
    part = jax.ShapeDtypeStruct(keep.shape[1:], BF16)
    own, *sends = pl.pallas_call(
        fold_kernel,
        out_shape=[jax.ShapeDtypeStruct(part.shape, F32)] + [part] * 3,
        in_specs=[SMEM] + [VMEM] * 2 + [ANY],
        out_specs=[VMEM] * 4,
        compiler_params=small,
        name="fold",
    )(here, keep, got, attn_out)
    parts = [swap(send, "dp", 2 * at + 2) for at, send in enumerate(sends)]
    attn_out = attend(beside_y, row_count - beside_y, attn_out, tie=own)
    moe_out = pl.pallas_call(
        finish_kernel,
        out_shape=jax.ShapeDtypeStruct(hidden_in.shape, BF16),
        in_specs=[VMEM] * 4,
        out_specs=VMEM,
        compiler_params=small,
        name="finish",
    )(own, *parts)
    return attn_out, moe_out


def experts_exchanged(hidden_in, ln_gain, route_ids, route_logits, w_gate, w_up, w_down):
    ranks = lax.axis_size("dp")
    row_count = hidden_in.shape[1]
    whole_rows = lax.all_gather(hidden_in, "rep", axis=2, tiled=True)
    values = whole_rows.astype(F32)
    mean_square = jnp.mean(values * values, axis=-1, keepdims=True)
    normed = (values * lax.rsqrt(mean_square + EPS) * ln_gain).astype(BF16)
    slots = place(route_ids)
    targets = route_ids * CAPACITY + slots
    expert_slots = jnp.arange(EXPERTS * CAPACITY, dtype=jnp.int32)
    hits = jnp.any(targets[:, None, :, :] == expert_slots[None, :, None, None], axis=-1)
    hits = hits.astype(BF16).reshape(STEPS, EXPERTS, CAPACITY, row_count)
    packed = jnp.einsum("secr,srd->escd", hits, normed, preferred_element_type=F32).astype(BF16)
    outgoing = jnp.broadcast_to(packed[None], (2,) + packed.shape).reshape(
        ranks, -1, packed.shape[-1]
    )
    incoming = lax.all_to_all(outgoing, "dp", split_axis=0, concat_axis=0, tiled=True)
    local_count = w_gate.shape[0]
    arrived = incoming.reshape(ranks, local_count, STEPS * CAPACITY, D)
    gate = jnp.einsum("nlrd,ldf->nlrf", arrived, w_gate, preferred_element_type=F32)
    upper = jnp.einsum("nlrd,ldf->nlrf", arrived, w_up, preferred_element_type=F32)
    hidden_part = (jax.nn.silu(gate) * upper).astype(BF16)
    hidden_all = lax.all_gather(hidden_part, "rep", axis=3, tiled=True)
    produced = jnp.einsum("nlrf,lfd->nlrd", hidden_all, w_down, preferred_element_type=F32)
    produced = produced.astype(BF16)
    returned = lax.all_to_all(
        produced.reshape(ranks, -1, produced.shape[-1]), "dp", split_axis=0, concat_axis=0, tiled=True
    )
    returned = returned.reshape(2, EXPERTS, STEPS, CAPACITY, -1).astype(F32)
    both_halves = returned[0] + returned[1]
    section_index = jnp.broadcast_to(
        jnp.arange(STEPS, dtype=jnp.int32)[:, None, None], route_ids.shape
    )
    picked = both_halves[route_ids, section_index, slots]
    weights = jax.nn.softmax(route_logits, axis=-1)
    return jnp.sum(weights[..., None] * picked, axis=2).astype(BF16)


def exchanged(
    q_raw, k_raw, v_raw, q_gain, k_gain, kv_pool, page_table, cache_len, out_pages, in_slots,
    hidden_in, ln_gain, route_ids, route_logits, w_gate, w_up, w_down,
):
    ranks = lax.axis_size("dp")
    pool = kv_pool.reshape(kv_pool.shape[0], -1, kv_pool.shape[3])
    leaving = pool[out_pages]
    arriving = lax.ppermute(leaving, "dp", [(i, (i + ranks // 2) % ranks) for i in range(ranks)])
    attn_out = attention(
        arriving, q_raw, k_raw, v_raw, q_gain, k_gain, pool, page_table, cache_len, in_slots,
        0, q_raw.shape[1],
    )
    moe_out = experts_exchanged(hidden_in, ln_gain, route_ids, route_logits, w_gate, w_up, w_down)
    return attn_out, moe_out


def local(*args):
    plan = gathered if (lax.axis_size("dp"), lax.axis_size("rep")) == (8, 4) else exchanged
    return plan(*args)


def solution(mesh):
    return jax.shard_map(
        local,
        mesh=mesh,
        in_specs=(
            P(None, "dp", "rep"),
            P(None, "dp", "rep"),
            P(None, "dp", "rep"),
            P(),
            P(),
            P("dp", None, None, "rep"),
            P("dp", None),
            P("dp"),
            P("dp"),
            P("dp"),
            P(None, "dp", "rep"),
            P(),
            P(None, "dp", None),
            P(None, "dp", None),
            P("dp", None, "rep"),
            P("dp", None, "rep"),
            P("dp", None, "rep"),
        ),
        out_specs=(P(None, "dp", "rep"), P(None, "dp", "rep")),
        check_vma=False,
    )
```
